256 devices in a mesh: dp: 32 (over y, z_lo, core), ctx: 8 (over x, z_hi).
Axes of the slice: x: 4, y: 4, z: 8 (z_hi: 2, z_lo: 4; z = z_hi * 4 + z_lo), core: 2. Of those that a mesh axis runs over, the one named last changes fastest.
Arguments:
- query_in: bfloat16 [32768, 4096], P(('dp', 'ctx')), may hold values from -5 to 5
- key_in: bfloat16 [32768, 4096], P(('dp', 'ctx')), may hold values from -5 to 5
- value_in: bfloat16 [32768, 4096], P(('dp', 'ctx')), may hold values from -5 to 5
- grad_out: bfloat16 [32768, 4096], P(('dp', 'ctx')), may hold values from -5 to 5
- filters: bfloat16 [32768, 4096], P('dp', 'ctx'), may hold values from -2 to 2
Outputs:
- gated_out: bfloat16 [32768, 4096], P(('dp', 'ctx'))
- grad_query: bfloat16 [32768, 4096], P(('dp', 'ctx'))
- grad_key: bfloat16 [32768, 4096], P(('dp', 'ctx'))
- grad_value: bfloat16 [32768, 4096], P(('dp', 'ctx'))
The draws below stay inside these ranges and needn't reach their ends.
All inputs are finite; a program needn't handle non-finite values.
Results may differ from the reference program's by a relative error of at most 0.0087.
Values may be sent and summed in bfloat16 or wider, within the bound.
No kernel may reach another device: no remote copies, remote signals or barrier semaphores. Data moves between devices by JAX's collectives and lax.ppermute only.
A program may use at most 128 MiB of HBM per device.

```python
import math
import jax
import jax.numpy as jnp
from jax import lax

CHANNELS = 4096
TOKENS = 32768
OUTER = 8
INNER = 128
N_DP = 32


def draw_filters(key, part):
    key = jax.random.fold_in(key, 7)
    key_rates, key_noise = jax.random.split(key)
    lowest_log = math.log(30.0)
    log_decay = jax.random.uniform(key_rates, (1, CHANNELS), jnp.float32, lowest_log, math.log(4.0 * TOKENS))
    decay_len = jnp.exp(log_decay)
    positions = jnp.arange(TOKENS, dtype=jnp.float32)[:, None]
    noise = jnp.clip(jax.random.normal(key_noise, (TOKENS, CHANNELS), jnp.float32), -4.0, 4.0)
    envelope = jnp.exp(-positions / decay_len) * jnp.sqrt(2.0 / decay_len)
    return (noise * envelope).astype(jnp.bfloat16)


def block_levels(own_key, dims, cuts, low, largest):
    def one(dim, parts):
        draws = jax.random.uniform(jax.random.fold_in(jax.random.fold_in(own_key, 6), dim), (parts,), jnp.float32, low / len(cuts), largest / len(cuts))
        return jnp.repeat(jnp.exp(draws), dims[dim] // parts).reshape((-1,) + (1,) * (len(dims) - dim - 1))

    level = one(*cuts[0])
    for cut in cuts[1:]:
        level = level * one(*cut)
    return level


def scatter_about(key, extent, width, reach, cuts=(), kind=jnp.bfloat16):
    gain = block_levels(key, extent, cuts, -0.22, 0.18) if cuts else 1.0
    result = jax.random.normal(key, extent, jnp.float32) * width * gain
    return jnp.minimum(jnp.maximum(result, -reach), reach).astype(kind)


def setup_inputs(seed: int = 0) -> dict:
    streams_of = jax.random.split(jax.random.key(seed), 6)
    query_in = scatter_about(streams_of[0], (TOKENS, CHANNELS), 1.0, 5.0, ((0, 256),))
    key_in = scatter_about(streams_of[1], (TOKENS, CHANNELS), 1.0, 5.0, ((0, 256),))
    value_in = scatter_about(streams_of[2], (TOKENS, CHANNELS), 1.0, 5.0, ((0, 256),))
    grad_out = scatter_about(streams_of[3], (TOKENS, CHANNELS), 1.0, 5.0, ((0, 256),))
    filters = draw_filters(jax.random.fold_in(streams_of[5], 71), 0)
    return {"query_in": query_in, "key_in": key_in, "value_in": value_in, "grad_out": grad_out, "filters": filters}


def angles(period, left_index, right_index, direction):
    phase_idx = (left_index[:, None] * right_index[None, :]) % period
    angle_rad = (direction * 2.0 * math.pi / period) * phase_idx.astype(jnp.float32)
    return jnp.cos(angle_rad), jnp.sin(angle_rad)


def complex_table(period, left_index, right_index, direction):
    cos_part, sin_part = angles(period, left_index, right_index, direction)
    return jnp.stack([jnp.stack([cos_part, -sin_part]), jnp.stack([sin_part, cos_part])]).astype(jnp.bfloat16)


def rotate_round(data, cos_part, sin_part):
    real_part = data[0]
    imag_part = data[1]
    return jnp.stack([real_part * cos_part - imag_part * sin_part, real_part * sin_part + imag_part * cos_part]).astype(jnp.bfloat16)


def apply_filter(filt_spec, gate_spec, grad_spec):
    conv_spec = jnp.stack([filt_spec[0] * gate_spec[0] - filt_spec[1] * gate_spec[1], filt_spec[0] * gate_spec[1] + filt_spec[1] * gate_spec[0]])
    corr_spec = jnp.stack([filt_spec[0] * grad_spec[0] + filt_spec[1] * grad_spec[1], filt_spec[0] * grad_spec[1] - filt_spec[1] * grad_spec[0]])
    return conv_spec.astype(jnp.bfloat16), corr_spec.astype(jnp.bfloat16)


def reference(query_in, key_in, value_in, grad_out, filters):
    gate_in = (key_in.astype(jnp.float32) * value_in.astype(jnp.float32)).astype(jnp.bfloat16)
    grad_conv = (grad_out.astype(jnp.float32) * query_in.astype(jnp.float32)).astype(jnp.bfloat16)
    length = filters.shape[0]
    block_count = N_DP
    row_count = length // block_count
    wave_count = 2 * block_count
    period = 2 * length
    outer_count = OUTER
    inner_count = INNER
    group_size = min(256, filters.shape[1])
    wave_idx = jnp.arange(wave_count, dtype=jnp.int32)
    block_idx = jnp.arange(block_count, dtype=jnp.int32)
    row_idx = jnp.arange(row_count, dtype=jnp.int32)
    outer_idx = jnp.arange(outer_count, dtype=jnp.int32)
    inner_idx = jnp.arange(inner_count, dtype=jnp.int32)
    fwd_cos, fwd_sin = angles(wave_count, wave_idx, block_idx, -1.0)
    section_fwd = jnp.stack([fwd_cos, fwd_sin]).astype(jnp.bfloat16)
    twist_fc, twist_fs = angles(period, wave_idx, row_idx, -1.0)
    outer_fwd = complex_table(outer_count, outer_idx, outer_idx, -1.0)
    mid_fc, mid_fs = angles(row_count, outer_idx, inner_idx, -1.0)
    inner_fwd = complex_table(inner_count, inner_idx, inner_idx, -1.0)
    inner_bwd = complex_table(inner_count, inner_idx, inner_idx, 1.0)
    mid_bc, mid_bs = angles(row_count, outer_idx, inner_idx, 1.0)
    outer_bwd = complex_table(outer_count, outer_idx, outer_idx, 1.0)
    twist_bc, twist_bs = angles(period, wave_idx, row_idx, 1.0)
    bwd_cos, bwd_sin = angles(wave_count, block_idx, wave_idx, 1.0)
    section_bwd = jnp.stack([bwd_cos, -bwd_sin]).astype(jnp.bfloat16)

    def forward(signal):
        values = signal.reshape(block_count, row_count, -1)
        mid = jnp.einsum("zkp,prc->zkrc", section_fwd, values, preferred_element_type=jnp.float32)
        part = rotate_round(mid, twist_fc[:, :, None], twist_fs[:, :, None])
        part = part.reshape(2, wave_count, outer_count, inner_count, -1)
        middle = jnp.einsum("zyka,ywavc->zwkvc", outer_fwd, part, preferred_element_type=jnp.float32)
        middle = rotate_round(middle, mid_fc[None, :, :, None], mid_fs[None, :, :, None])
        return jnp.einsum("zyjv,ywkvc->zwkjc", inner_fwd, middle, preferred_element_type=jnp.float32)

    def backward(spectrum):
        unmixed = jnp.einsum("zyvj,ywkjc->zwkvc", inner_bwd, spectrum, preferred_element_type=jnp.float32)
        unmixed = rotate_round(unmixed, mid_bc[None, :, :, None], mid_bs[None, :, :, None])
        back = jnp.einsum("zyak,ywkvc->zwavc", outer_bwd, unmixed, preferred_element_type=jnp.float32).astype(jnp.bfloat16)
        back = back.reshape(2, wave_count, row_count, -1).astype(jnp.float32)
        spun = rotate_round(back, twist_bc[:, :, None], twist_bs[:, :, None])
        values = jnp.einsum("zpk,zkrc->prc", section_bwd, spun, preferred_element_type=jnp.float32)
        return (values * (1.0 / period)).reshape(length, -1).astype(jnp.bfloat16)

    def regroup(array):
        return array.reshape(length, -1, group_size).transpose(1, 0, 2)

    def convolve(pieces):
        filt_part, gate_part, grad_part = pieces
        conv_spec, corr_spec = apply_filter(forward(filt_part), forward(gate_part), forward(grad_part))
        return backward(conv_spec), backward(corr_spec)

    conv_groups, corr_groups = lax.map(convolve, (regroup(filters), regroup(gate_in), regroup(grad_conv)))
    conv_out = conv_groups.transpose(1, 0, 2).reshape(length, -1).astype(jnp.float32)
    corr_out = corr_groups.transpose(1, 0, 2).reshape(length, -1).astype(jnp.float32)
    gated_out = (query_in.astype(jnp.float32) * conv_out).astype(jnp.bfloat16)
    grad_query = (grad_out.astype(jnp.float32) * conv_out).astype(jnp.bfloat16)
    grad_key = (corr_out * value_in.astype(jnp.float32)).astype(jnp.bfloat16)
    grad_value = (corr_out * key_in.astype(jnp.float32)).astype(jnp.bfloat16)
    return (gated_out, grad_query, grad_key, grad_value)
```

```python
import functools

import jax
import jax.numpy as jnp
import ml_dtypes
import numpy as np
from jax import lax
from jax.experimental import pallas as pl
from jax.experimental.pallas import tpu as pltpu
from jax.sharding import PartitionSpec as P

LANES = 128


def tables(length):
    rows = length // LANES
    period = 2 * length
    freq = np.arange(rows) + 0.5
    outer = 2.0 * np.pi / (2 * rows) * np.outer(freq, np.arange(rows))
    inner = 2.0 * np.pi / LANES * (np.outer(np.arange(LANES), np.arange(LANES)) % LANES)
    spin = 2.0 * np.pi / period * np.outer(freq, np.arange(LANES))
    cos, sin = np.cos(inner), np.sin(inner)
    kind = ml_dtypes.bfloat16
    outer_fwd = np.concatenate([np.cos(outer), -np.sin(outer)], axis=0).astype(kind)
    inner_fwd = np.block([[cos, -sin], [sin, cos]]).astype(kind)
    inner_bwd = np.block([[cos, sin], [-sin, cos]]).astype(kind)
    scale = np.float32(2.0 / period)
    outer_bwd = np.concatenate([np.cos(outer).T, -np.sin(outer).T], axis=1).astype(kind)
    outer_bwd = (outer_bwd.astype(np.float32) * scale).astype(kind)
    spin_cos = np.cos(spin).astype(np.float32)
    spin_sin = np.sin(spin).astype(np.float32)
    return outer_fwd, inner_fwd, inner_bwd, outer_bwd, spin_cos, spin_sin


def pack_kernel(query, key, value, grad, filt, out, lined, spread):
    group = pl.program_id(0)
    width = query.shape[1]
    owners = out.shape[0]
    per_owner = out.shape[2]
    pairs = (key, value), (grad, query)
    for slot, (left, right) in enumerate(pairs):
        prod = left[...].astype(jnp.float32) * right[...].astype(jnp.float32)
        lined[...] = prod.T
        for j in range(2):
            spread[slot, pl.ds(2 * group + j, owners, stride=per_owner), :] = lined[
                pl.ds(j, owners, stride=2), :
            ]
    spread[2, pl.ds(group, width, stride=per_owner // 2), :] = filt[...].astype(jnp.float32).T

    @pl.when(group == pl.num_programs(0) - 1)
    def _():
        for slot in range(3):
            out[:, slot] = (
                spread[slot].reshape(owners, per_owner, LANES).astype(jnp.bfloat16)
            )


def pack(query, key, value, grad, filt, owners):
    tokens, channels = query.shape
    groups = channels // filt.shape[1]
    width = filt.shape[1]
    per_owner = channels // owners
    column = pl.BlockSpec((tokens, width), lambda i: (0, i))
    return pl.pallas_call(
        pack_kernel,
        grid=(groups,),
        in_specs=[column, column, column, column, pl.BlockSpec((tokens, width), lambda i: (i, 0))],
        out_specs=pl.BlockSpec((owners, 3, per_owner, LANES), lambda i: (0, 0, 0, 0)),
        out_shape=jax.ShapeDtypeStruct((owners, 3, per_owner, LANES), jnp.bfloat16),
        scratch_shapes=[
            pltpu.VMEM((width, LANES), jnp.float32),
            pltpu.VMEM((3, owners * per_owner, LANES), jnp.float32),
        ],
        compiler_params=pltpu.CompilerParams(vmem_limit_bytes=48 << 20),
    )(query, key, value, grad, filt)


def mix_kernel(blocks, outer_fwd, inner_fwd, inner_bwd, outer_bwd, cos, sin, out, wide, done):
    blocks_p, groups, _, per_owner, _ = blocks.shape
    rows = blocks_p * groups
    for slot in range(2):
        wide[slot] = (
            blocks[:, :, slot].astype(jnp.float32).reshape(rows * per_owner, LANES)
        )

    def dot(left, right):
        return jnp.dot(left, right, preferred_element_type=jnp.float32)

    def forward(pair):
        mid = dot(outer_fwd[...], jnp.concatenate(pair, axis=1).astype(jnp.bfloat16))
        result = []
        for j in range(2):
            real = mid[:rows, j * LANES : (j + 1) * LANES]
            imag = mid[rows:, j * LANES : (j + 1) * LANES]
            spun = jnp.concatenate(
                [real * cos[...] + imag * sin[...], imag * cos[...] - real * sin[...]], axis=1
            ).astype(jnp.bfloat16)
            both = dot(spun, inner_fwd[...])
            result.append((both[:, :LANES], both[:, LANES:]))
        return result

    def backward(pair):
        spun = []
        for real, imag in pair:
            spec = jnp.concatenate([real, imag], axis=1).astype(jnp.bfloat16)
            both = dot(spec, inner_bwd[...])
            real, imag = both[:, :LANES], both[:, LANES:]
            spun.append(
                jnp.concatenate(
                    [real * cos[...] - imag * sin[...], real * sin[...] + imag * cos[...]], axis=0
                ).astype(jnp.bfloat16)
            )
        return dot(outer_bwd[...], jnp.concatenate(spun, axis=1))

    def step(group, carry):
        filt = blocks[:, group, 2].astype(jnp.float32)
        half = per_owner // 2
        filt_spec = forward([filt[:, j * half : (j + 1) * half].reshape(rows, LANES) for j in range(2)])
        for slot in range(2):
            spec = forward(
                [wide[slot, pl.ds(2 * group + j, rows, stride=per_owner), :] for j in range(2)]
            )
            mixed = []
            for (fr, fi), (gr, gi) in zip(filt_spec, spec):
                if slot == 0:
                    mixed.append((fr * gr - fi * gi, fr * gi + fi * gr))
                else:
                    mixed.append((fr * gr + fi * gi, fr * gi - fi * gr))
            result = backward(mixed)
            for j in range(2):
                done[slot, pl.ds(2 * group + j, rows, stride=per_owner), :] = result[
                    :, j * LANES : (j + 1) * LANES
                ]
        return carry

    lax.fori_loop(0, groups, step, 0)
    for slot in range(2):
        out[:, slot] = done[slot].reshape(rows, per_owner, LANES).astype(jnp.bfloat16)


def mix(blocks, groups):
    rows, _, per_owner, _ = blocks.shape
    consts = [jnp.asarray(t) for t in tables(rows * LANES)]
    return pl.pallas_call(
        mix_kernel,
        out_shape=jax.ShapeDtypeStruct((rows, 2, per_owner, LANES), jnp.bfloat16),
        scratch_shapes=[
            pltpu.VMEM((2, rows * per_owner, LANES), jnp.float32),
            pltpu.VMEM((2, rows * per_owner, LANES), jnp.float32),
        ],
        compiler_params=pltpu.CompilerParams(vmem_limit_bytes=56 << 20),
    )(blocks.reshape(rows // groups, groups, 3, per_owner, LANES), *consts)


def gate_kernel(sums, query, key, value, grad, gated, grad_query, grad_key, grad_value, wide, lined):
    group = pl.program_id(0)
    owners, _, per_owner, _ = sums.shape

    @pl.when(group == 0)
    def _():
        for slot in range(2):
            wide[slot] = sums[:, slot].astype(jnp.float32).reshape(owners * per_owner, LANES)

    uses = ((query, gated), (grad, grad_query)), ((value, grad_key), (key, grad_value))
    for slot in range(2):
        for j in range(2):
            lined[pl.ds(j, owners, stride=2), :] = wide[
                slot, pl.ds(2 * group + j, owners, stride=per_owner), :
            ]
        tokens = lined[...].T
        for source, target in uses[slot]:
            target[...] = (source[...].astype(jnp.float32) * tokens).astype(jnp.bfloat16)


def gate(sums, query, key, value, grad, width):
    tokens, channels = query.shape
    owners, _, per_owner, _ = sums.shape
    groups = channels // width
    column = pl.BlockSpec((tokens, width), lambda i: (0, i))
    return pl.pallas_call(
        gate_kernel,
        grid=(groups,),
        in_specs=[pl.BlockSpec(sums.shape, lambda i: (0, 0, 0, 0))] + [column] * 4,
        out_specs=[column] * 4,
        out_shape=[jax.ShapeDtypeStruct((tokens, channels), jnp.bfloat16)] * 4,
        scratch_shapes=[
            pltpu.VMEM((2, owners * per_owner, LANES), jnp.float32),
            pltpu.VMEM((width, LANES), jnp.float32),
        ],
        compiler_params=pltpu.CompilerParams(vmem_limit_bytes=48 << 20),
    )(sums, query, key, value, grad)


def body(query_in, key_in, value_in, grad_out, filters):
    axes = ("dp", "ctx")
    groups = lax.axis_size("ctx")
    owners = lax.axis_size("dp") * groups
    packed = pack(query_in, key_in, value_in, grad_out, filters, owners)
    blocks = lax.all_to_all(packed, axes, split_axis=0, concat_axis=0, tiled=True)
    mixed = mix(blocks, groups)
    sums = lax.all_to_all(mixed, axes, split_axis=0, concat_axis=0, tiled=True)
    return tuple(gate(sums, query_in, key_in, value_in, grad_out, filters.shape[1]))


def solution(mesh):
    tokens = P(("dp", "ctx"), None)
    return jax.shard_map(
        body,
        mesh=mesh,
        in_specs=(tokens, tokens, tokens, tokens, P("dp", "ctx")),
        out_specs=(tokens, tokens, tokens, tokens),
        check_vma=False,
    )
```

```python
import jax
import jax.numpy as jnp
import ml_dtypes
import numpy as np
from jax import lax
from jax.experimental import pallas as pl
from jax.experimental.pallas import tpu as pltpu
from jax.sharding import PartitionSpec as P

LANES = 128


def tables(length):
    rows = length // LANES
    period = 2 * length
    freq = np.arange(rows) + 0.5
    outer = 2.0 * np.pi / (2 * rows) * np.outer(freq, np.arange(rows))
    inner = 2.0 * np.pi / LANES * (np.outer(np.arange(LANES), np.arange(LANES)) % LANES)
    spin = 2.0 * np.pi / period * np.outer(freq, np.arange(LANES))
    cos, sin = np.cos(inner), np.sin(inner)
    kind = ml_dtypes.bfloat16
    outer_fwd = np.concatenate([np.cos(outer), -np.sin(outer)], axis=0).astype(kind)
    inner_fwd = np.block([[cos, -sin], [sin, cos]]).astype(kind)
    inner_bwd = np.block([[cos, sin], [-sin, cos]]).astype(kind)
    scale = np.float32(2.0 / period)
    outer_bwd = np.concatenate([np.cos(outer).T, -np.sin(outer).T], axis=1).astype(kind)
    outer_bwd = (outer_bwd.astype(np.float32) * scale).astype(kind)
    spin_cos = np.cos(spin).astype(np.float32)
    spin_sin = np.sin(spin).astype(np.float32)
    return outer_fwd, inner_fwd, inner_bwd, outer_bwd, spin_cos, spin_sin


def pack_kernel(query, key, value, grad, filt, out, raw, raw_filt, spread, ready, sems, out_sems):
    owners, _, per_owner, _ = out.shape
    half = per_owner // 2
    load_filt = pltpu.make_async_copy(filt, raw_filt, sems.at[4])
    load_filt.start()
    loads = []
    for i, source in enumerate((key, value, grad, query)):
        loads.append(pltpu.make_async_copy(source, raw.at[i], sems.at[i]))
        loads[-1].start()
    stores = []

    def send(slot, first, count):
        some = slice(first, first + count)
        lines = spread[slot, first * per_owner : (first + count) * per_owner]
        ready[slot, some] = lines.reshape(count, per_owner, LANES).astype(jnp.bfloat16)
        stores.append(
            pltpu.make_async_copy(
                ready.at[slot, some], out.at[some, slot], out_sems.at[len(stores)]
            )
        )
        stores[-1].start()

    load_filt.wait()
    for j in range(2):
        for a in range(half):
            lines = raw_filt[a * LANES : (a + 1) * LANES, j * owners : (j + 1) * owners]
            spread[2, pl.ds(j * half + a, owners, stride=per_owner), :] = lines.astype(jnp.float32).T
    send(2, 0, owners)
    for slot in range(2):
        loads[2 * slot].wait()
        loads[2 * slot + 1].wait()
        for i in range(per_owner):
            columns = slice(i * owners, (i + 1) * owners)
            prod = raw[2 * slot, :, columns].astype(jnp.float32) * raw[
                2 * slot + 1, :, columns
            ].astype(jnp.float32)
            spread[slot, pl.ds(i, owners, stride=per_owner), :] = prod.T
        if slot == 0:
            send(slot, 0, owners)
        else:
            for part in range(4):
                send(slot, part * (owners // 4), owners // 4)
    for store in stores:
        store.wait()


def pack(query, key, value, grad, filt, owners):
    tokens, channels = query.shape
    per_owner = channels // owners
    return pl.pallas_call(
        pack_kernel,
        in_specs=[pl.BlockSpec(memory_space=pltpu.HBM)] * 5,
        out_specs=pl.BlockSpec(memory_space=pltpu.HBM),
        out_shape=jax.ShapeDtypeStruct((owners, 3, per_owner, LANES), jnp.bfloat16),
        scratch_shapes=[
            pltpu.VMEM((4, tokens, channels), jnp.bfloat16),
            pltpu.VMEM(filt.shape, jnp.bfloat16),
            pltpu.VMEM((3, owners * per_owner, LANES), jnp.float32),
            pltpu.VMEM((3, owners, per_owner, LANES), jnp.bfloat16),
            pltpu.SemaphoreType.DMA((5,)),
            pltpu.SemaphoreType.DMA((6,)),
        ],
        compiler_params=pltpu.CompilerParams(vmem_limit_bytes=60 << 20),
    )(query, key, value, grad, filt)


def mix_kernel(blocks, outer_fwd, inner_fwd, inner_bwd, outer_bwd, cos, sin, out, wide, done):
    blocks_p, groups, _, per_owner, _ = blocks.shape
    rows = blocks_p * groups
    half = per_owner // 2
    for slot in range(2):
        wide[slot] = (
            blocks[:, :, slot].astype(jnp.float32).reshape(rows * per_owner, LANES)
        )

    def dot(left, right):
        return jnp.dot(left, right, preferred_element_type=jnp.float32)

    def step(group, carry):
        filt = blocks[:, group, 2].astype(jnp.float32)
        lines = [filt[:, j * half : (j + 1) * half].reshape(rows, LANES) for j in range(2)]
        for slot in range(2):
            for j in range(2):
                lines.append(wide[slot, pl.ds(2 * group + j, rows, stride=per_owner), :])
        mid = dot(outer_fwd[...], jnp.concatenate(lines, axis=1).astype(jnp.bfloat16))
        spun = []
        for i in range(6):
            real = mid[:rows, i * LANES : (i + 1) * LANES]
            imag = mid[rows:, i * LANES : (i + 1) * LANES]
            spun.append(jnp.concatenate(
                [real * cos[...] + imag * sin[...], imag * cos[...] - real * sin[...]], axis=1
            ).astype(jnp.bfloat16))
        both = dot(jnp.concatenate(spun, axis=0), inner_fwd[...])
        spec = [
            (both[i * rows : (i + 1) * rows, :LANES], both[i * rows : (i + 1) * rows, LANES:])
            for i in range(6)
        ]
        mixed = []
        for slot in range(2):
            for j in range(2):
                (fr, fi), (gr, gi) = spec[j], spec[2 + 2 * slot + j]
                if slot == 0:
                    real, imag = fr * gr - fi * gi, fr * gi + fi * gr
                else:
                    real, imag = fr * gr + fi * gi, fr * gi - fi * gr
                mixed.append(jnp.concatenate([real, imag], axis=1).astype(jnp.bfloat16))
        both = dot(jnp.concatenate(mixed, axis=0), inner_bwd[...])
        spun = []
        for i in range(4):
            real = both[i * rows : (i + 1) * rows, :LANES]
            imag = both[i * rows : (i + 1) * rows, LANES:]
            spun.append(jnp.concatenate(
                [real * cos[...] - imag * sin[...], real * sin[...] + imag * cos[...]], axis=0
            ).astype(jnp.bfloat16))
        result = dot(outer_bwd[...], jnp.concatenate(spun, axis=1))
        for slot in range(2):
            for j in range(2):
                i = 2 * slot + j
                done[slot, pl.ds(2 * group + j, rows, stride=per_owner), :] = result[
                    :, i * LANES : (i + 1) * LANES
                ]
        return carry

    lax.fori_loop(0, groups, step, 0, unroll=True)
    for slot in range(2):
        out[:, slot] = done[slot].reshape(rows, per_owner, LANES).astype(jnp.bfloat16)


def mix(blocks, groups):
    rows, _, per_owner, _ = blocks.shape
    consts = [jnp.asarray(t) for t in tables(rows * LANES)]
    return pl.pallas_call(
        mix_kernel,
        out_shape=jax.ShapeDtypeStruct((rows, 2, per_owner, LANES), jnp.bfloat16),
        scratch_shapes=[
            pltpu.VMEM((2, rows * per_owner, LANES), jnp.float32),
            pltpu.VMEM((2, rows * per_owner, LANES), jnp.float32),
        ],
        compiler_params=pltpu.CompilerParams(vmem_limit_bytes=24 << 20),
    )(blocks.reshape(rows // groups, groups, 3, per_owner, LANES), *consts)


def gate_kernel(sums, query, key, value, grad, gated, grad_query, grad_key, grad_value, wide, ready, sems):
    owners, _, per_owner, _ = sums.shape
    channels = query.shape[1]
    width = 2 * owners
    uses = ((query, gated), (grad, grad_query)), ((value, grad_key), (key, grad_value))
    stores = []
    for slot in range(2):
        wide[slot] = sums[:, slot].astype(jnp.float32).reshape(owners * per_owner, LANES)
        for group in range(channels // width):
            for j in range(2):
                i = 2 * group + j
                columns = slice(i * owners, (i + 1) * owners)
                tokens = wide[slot, pl.ds(i, owners, stride=per_owner), :].T
                for k, (source, _) in enumerate(uses[slot]):
                    ready[2 * slot + k, :, columns] = (
                        source[:, columns].astype(jnp.float32) * tokens
                    ).astype(jnp.bfloat16)
            columns = pl.ds(group * width, width)
            for k, (_, target) in enumerate(uses[slot]):
                stores.append(
                    pltpu.make_async_copy(
                        ready.at[2 * slot + k, :, columns],
                        target.at[:, columns],
                        sems.at[len(stores)],
                    )
                )
                stores[-1].start()
    for store in stores:
        store.wait()


def gate(sums, query, key, value, grad, width):
    tokens, channels = query.shape
    owners, _, per_owner, _ = sums.shape
    whole = pl.BlockSpec(memory_space=pltpu.VMEM)
    return pl.pallas_call(
        gate_kernel,
        in_specs=[whole] * 5,
        out_specs=[pl.BlockSpec(memory_space=pltpu.HBM)] * 4,
        out_shape=[jax.ShapeDtypeStruct((tokens, channels), jnp.bfloat16)] * 4,
        scratch_shapes=[
            pltpu.VMEM((2, owners * per_owner, LANES), jnp.float32),
            pltpu.VMEM((4, tokens, channels), jnp.bfloat16),
            pltpu.SemaphoreType.DMA((4 * channels // width,)),
        ],
        compiler_params=pltpu.CompilerParams(vmem_limit_bytes=24 << 20),
    )(sums, query, key, value, grad)


def body(query_in, key_in, value_in, grad_out, filters):
    axes = ("dp", "ctx")
    groups = lax.axis_size("ctx")
    owners = lax.axis_size("dp") * groups
    packed = pack(query_in, key_in, value_in, grad_out, filters, owners)
    blocks = lax.all_to_all(packed, axes, split_axis=0, concat_axis=0, tiled=True)
    mixed = mix(blocks, groups)
    sums = lax.all_to_all(mixed, axes, split_axis=0, concat_axis=0, tiled=True)
    return tuple(gate(sums, query_in, key_in, value_in, grad_out, filters.shape[1]))


def solution(mesh):
    tokens = P(("dp", "ctx"), None)
    return jax.shard_map(
        body,
        mesh=mesh,
        in_specs=(tokens, tokens, tokens, tokens, P("dp", "ctx")),
        out_specs=(tokens, tokens, tokens, tokens),
        check_vma=False,
    )
```

```python
import jax
import jax.numpy as jnp
import ml_dtypes
import numpy as np
from jax import lax
from jax.experimental import pallas as pl
from jax.experimental.pallas import tpu as pltpu
from jax.sharding import PartitionSpec as P

LANES = 128
TILE = 16
PITCH = 24


def tables(length):
    rows = length // LANES
    period = 2 * length
    freq = np.arange(rows) + 0.5
    outer = 2.0 * np.pi / (2 * rows) * np.outer(freq, np.arange(rows))
    inner = 2.0 * np.pi / LANES * (np.outer(np.arange(LANES), np.arange(LANES)) % LANES)
    spin = 2.0 * np.pi / period * np.outer(freq, np.arange(LANES))
    cos, sin = np.cos(inner), np.sin(inner)
    kind = ml_dtypes.bfloat16
    both = np.stack([np.cos(outer), -np.sin(outer)], axis=1)
    both = both.reshape(rows // TILE, TILE, 2, rows).transpose(0, 2, 1, 3).reshape(2 * rows, rows)
    outer_fwd = both.astype(kind)
    inner_fwd = np.block([[cos, -sin], [sin, cos]]).astype(kind)
    inner_bwd = np.block([[cos, sin], [-sin, cos]]).astype(kind)
    scale = np.float32(2.0 / period)
    outer_bwd = (both.T.astype(kind).astype(np.float32) * scale).astype(kind)
    spin_cos = np.cos(spin).astype(np.float32)
    spin_sin = np.sin(spin).astype(np.float32)
    return outer_fwd, inner_fwd, inner_bwd, outer_bwd, spin_cos, spin_sin


def pack_kernel(query, key, value, grad, filt, out, raw, raw_filt, spread, ready, sems, out_sems):
    owners, _, per_owner, _ = out.shape
    half = per_owner // 2
    load_filt = pltpu.make_async_copy(filt, raw_filt, sems.at[4])
    load_filt.start()
    loads = []
    for i, source in enumerate((key, value, grad, query)):
        loads.append(pltpu.make_async_copy(source, raw.at[i], sems.at[i]))
        loads[-1].start()
    stores = []

    def send(slot, first, count):
        some = slice(first, first + count)
        lines = spread[slot, first * PITCH : (first + count) * PITCH]
        lines = lines.reshape(count, PITCH, LANES)[:, :per_owner]
        ready[slot, some] = lines.astype(jnp.bfloat16)
        stores.append(
            pltpu.make_async_copy(
                ready.at[slot, some], out.at[some, slot], out_sems.at[len(stores)]
            )
        )
        stores[-1].start()

    load_filt.wait()
    for j in range(2):
        for a in range(half):
            lines = raw_filt[a * LANES : (a + 1) * LANES, j * owners : (j + 1) * owners]
            spread[2, pl.ds(j * half + a, owners, stride=PITCH), :] = lines.astype(jnp.float32).T
    send(2, 0, owners)
    for slot in range(2):
        loads[2 * slot].wait()
        loads[2 * slot + 1].wait()
        for i in range(per_owner):
            columns = slice(i * owners, (i + 1) * owners)
            prod = raw[2 * slot, :, columns].astype(jnp.float32) * raw[
                2 * slot + 1, :, columns
            ].astype(jnp.float32)
            spread[slot, pl.ds(i, owners, stride=PITCH), :] = prod.T
        if slot == 0:
            send(slot, 0, owners)
        else:
            for part in range(4):
                send(slot, part * (owners // 4), owners // 4)
    for store in stores:
        store.wait()


def pack(query, key, value, grad, filt, owners):
    tokens, channels = query.shape
    per_owner = channels // owners
    return pl.pallas_call(
        pack_kernel,
        in_specs=[pl.BlockSpec(memory_space=pltpu.HBM)] * 5,
        out_specs=pl.BlockSpec(memory_space=pltpu.HBM),
        out_shape=jax.ShapeDtypeStruct((owners, 3, per_owner, LANES), jnp.bfloat16),
        scratch_shapes=[
            pltpu.VMEM((4, tokens, channels), jnp.bfloat16),
            pltpu.VMEM(filt.shape, jnp.bfloat16),
            pltpu.VMEM((3, owners * PITCH, LANES), jnp.float32),
            pltpu.VMEM((3, owners, per_owner, LANES), jnp.bfloat16),
            pltpu.SemaphoreType.DMA((5,)),
            pltpu.SemaphoreType.DMA((6,)),
        ],
        compiler_params=pltpu.CompilerParams(vmem_limit_bytes=60 << 20),
    )(query, key, value, grad, filt)


def mix_kernel(blocks, outer_fwd, inner_fwd, inner_bwd, outer_bwd, cos, sin, out, wide, done):
    blocks_p, groups, _, per_owner, _ = blocks.shape
    rows = blocks_p * groups
    half = per_owner // 2
    for slot in range(2):
        lines = blocks[:, :, slot].astype(jnp.float32).reshape(rows, per_owner, LANES)
        wide[slot, :, :per_owner] = lines

    wide = wide.reshape(2, rows * PITCH, LANES)
    flat = done.reshape(2, rows * PITCH, LANES)

    def dot(left, right):
        return jnp.dot(left, right, preferred_element_type=jnp.float32)

    def step(group, carry):
        filt = blocks[:, group, 2].astype(jnp.float32)
        lines = [filt[:, j * half : (j + 1) * half].reshape(rows, LANES) for j in range(2)]
        for slot in range(2):
            for j in range(2):
                lines.append(wide[slot, pl.ds(2 * group + j, rows, stride=PITCH), :])
        mids = []
        for i in range(3):
            pair = jnp.concatenate(lines[2 * i : 2 * i + 2], axis=1).astype(jnp.bfloat16)
            mid = dot(outer_fwd[...], pair).reshape(rows // TILE, 2, TILE, 2 * LANES)
            mids += [mid[..., :LANES], mid[..., LANES:]]
        c, s = cos[...].reshape(rows // TILE, TILE, LANES), sin[...].reshape(rows // TILE, TILE, LANES)
        spun = []
        for mid in mids:
            real, imag = mid[:, 0], mid[:, 1]
            spun.append(jnp.concatenate(
                [real * c + imag * s, imag * c - real * s], axis=2
            ).reshape(rows, 2 * LANES).astype(jnp.bfloat16))
        spec = []
        for i in range(3):
            both = dot(jnp.concatenate(spun[2 * i : 2 * i + 2], axis=0), inner_fwd[...])
            spec += [(both[:rows, :LANES], both[:rows, LANES:]), (both[rows:, :LANES], both[rows:, LANES:])]
        mixed = []
        for slot in range(2):
            for j in range(2):
                (fr, fi), (gr, gi) = spec[j], spec[2 + 2 * slot + j]
                if slot == 0:
                    real, imag = fr * gr - fi * gi, fr * gi + fi * gr
                else:
                    real, imag = fr * gr + fi * gi, fr * gi - fi * gr
                mixed.append(jnp.concatenate([real, imag], axis=1).astype(jnp.bfloat16))
        boths = [dot(m, inner_bwd[...]) for m in mixed]
        spun = []
        for both in boths:
            both = both.reshape(rows // TILE, TILE, 2 * LANES)
            real, imag = both[..., :LANES], both[..., LANES:]
            spun.append(jnp.stack(
                [real * c - imag * s, real * s + imag * c], axis=1
            ).reshape(2 * rows, LANES).astype(jnp.bfloat16))
        for slot in range(2):
            result = dot(outer_bwd[...], jnp.concatenate(spun[2 * slot : 2 * slot + 2], axis=1))
            for j in range(2):
                flat[slot, pl.ds(2 * group + j, rows, stride=PITCH), :] = result[
                    :, j * LANES : (j + 1) * LANES
                ]
        return carry

    lax.fori_loop(0, groups, step, 0, unroll=True)
    for slot in range(2):
        out[:, slot] = done[slot, :, :per_owner].astype(jnp.bfloat16)


def mix(blocks, groups):
    rows, _, per_owner, _ = blocks.shape
    consts = [jnp.asarray(t) for t in tables(rows * LANES)]
    return pl.pallas_call(
        mix_kernel,
        out_shape=jax.ShapeDtypeStruct((rows, 2, per_owner, LANES), jnp.bfloat16),
        scratch_shapes=[
            pltpu.VMEM((2, rows, PITCH, LANES), jnp.float32),
            pltpu.VMEM((2, rows, PITCH, LANES), jnp.float32),
        ],
        compiler_params=pltpu.CompilerParams(vmem_limit_bytes=32 << 20),
    )(blocks.reshape(rows // groups, groups, 3, per_owner, LANES), *consts)


def gate_kernel(sums, query, key, value, grad, gated, grad_query, grad_key, grad_value, wide, ready, sems):
    owners, _, per_owner, _ = sums.shape
    channels = query.shape[1]
    width = 2 * owners
    uses = ((query, gated), (grad, grad_query)), ((value, grad_key), (key, grad_value))
    stores = []
    flat = wide.reshape(2, owners * PITCH, LANES)
    for slot in range(2):
        wide[slot, :, :per_owner] = sums[:, slot].astype(jnp.float32)
        for group in range(channels // width):
            for j in range(2):
                i = 2 * group + j
                columns = slice(i * owners, (i + 1) * owners)
                tokens = flat[slot, pl.ds(i, owners, stride=PITCH), :].T
                for k, (source, _) in enumerate(uses[slot]):
                    ready[2 * slot + k, :, columns] = (
                        source[:, columns].astype(jnp.float32) * tokens
                    ).astype(jnp.bfloat16)
            columns = pl.ds(group * width, width)
            for k, (_, target) in enumerate(uses[slot]):
                stores.append(
                    pltpu.make_async_copy(
                        ready.at[2 * slot + k, :, columns],
                        target.at[:, columns],
                        sems.at[len(stores)],
                    )
                )
                stores[-1].start()
    for store in stores:
        store.wait()


def gate(sums, query, key, value, grad, width):
    tokens, channels = query.shape
    owners, _, per_owner, _ = sums.shape
    whole = pl.BlockSpec(memory_space=pltpu.VMEM)
    return pl.pallas_call(
        gate_kernel,
        in_specs=[whole] * 5,
        out_specs=[pl.BlockSpec(memory_space=pltpu.HBM)] * 4,
        out_shape=[jax.ShapeDtypeStruct((tokens, channels), jnp.bfloat16)] * 4,
        scratch_shapes=[
            pltpu.VMEM((2, owners, PITCH, LANES), jnp.float32),
            pltpu.VMEM((4, tokens, channels), jnp.bfloat16),
            pltpu.SemaphoreType.DMA((4 * channels // width,)),
        ],
        compiler_params=pltpu.CompilerParams(vmem_limit_bytes=24 << 20),
    )(sums, query, key, value, grad)


def body(query_in, key_in, value_in, grad_out, filters):
    axes = ("dp", "ctx")
    groups = lax.axis_size("ctx")
    owners = lax.axis_size("dp") * groups
    packed = pack(query_in, key_in, value_in, grad_out, filters, owners)
    blocks = lax.all_to_all(packed, axes, split_axis=0, concat_axis=0, tiled=True)
    mixed = mix(blocks, groups)
    sums = lax.all_to_all(mixed, axes, split_axis=0, concat_axis=0, tiled=True)
    return tuple(gate(sums, query_in, key_in, value_in, grad_out, filters.shape[1]))


def solution(mesh):
    tokens = P(("dp", "ctx"), None)
    return jax.shard_map(
        body,
        mesh=mesh,
        in_specs=(tokens, tokens, tokens, tokens, P("dp", "ctx")),
        out_specs=(tokens, tokens, tokens, tokens),
        check_vma=False,
    )
```

```python
import jax
import jax.numpy as jnp
import ml_dtypes
import numpy as np
from jax import lax
from jax.experimental import pallas as pl
from jax.experimental.pallas import tpu as pltpu
from jax.sharding import PartitionSpec as P

LANES = 128
TILE = 16
PITCH = 24


def tables(length):
    rows = length // LANES
    period = 2 * length
    freq = np.arange(rows) + 0.5
    outer = 2.0 * np.pi / (2 * rows) * np.outer(freq, np.arange(rows))
    inner = 2.0 * np.pi / LANES * (np.outer(np.arange(LANES), np.arange(LANES)) % LANES)
    spin = 2.0 * np.pi / period * np.outer(freq, np.arange(LANES))
    cos, sin = np.cos(inner), np.sin(inner)
    kind = ml_dtypes.bfloat16
    both = np.stack([np.cos(outer), -np.sin(outer)], axis=1)
    both = both.reshape(rows // TILE, TILE, 2, rows).transpose(0, 2, 1, 3).reshape(2 * rows, rows)
    outer_fwd = both.astype(kind)
    inner_fwd = np.block([[cos, -sin], [sin, cos]]).astype(kind)
    inner_bwd = np.block([[cos, sin], [-sin, cos]]).astype(kind)
    scale = np.float32(2.0 / period)
    outer_bwd = (both.T.astype(kind).astype(np.float32) * scale).astype(kind)
    spin_cos = np.cos(spin).astype(np.float32)
    spin_sin = np.sin(spin).astype(np.float32)
    return outer_fwd, inner_fwd, inner_bwd, outer_bwd, spin_cos, spin_sin


def pack_kernel(query, key, value, grad, filt, out, raw, raw_filt, spread, sems):
    owners, _, per_owner, _ = out.shape
    half = per_owner // 2
    load_filt = pltpu.make_async_copy(filt, raw_filt, sems.at[4])
    load_filt.start()
    loads = []
    for i, source in enumerate((key, value, grad, query)):
        loads.append(pltpu.make_async_copy(source, raw.at[i], sems.at[i]))
        loads[-1].start()

    def send(slot, first, count):
        some = slice(first, first + count)
        lines = spread[slot, first * PITCH : (first + count) * PITCH]
        lines = lines.reshape(count, PITCH, LANES)[:, :per_owner]
        out[some, slot] = lines.astype(jnp.bfloat16)

    load_filt.wait()
    for j in range(2):
        for a in range(half):
            lines = raw_filt[a * LANES : (a + 1) * LANES, j * owners : (j + 1) * owners]
            spread[2, pl.ds(j * half + a, owners, stride=PITCH), :] = lines.astype(jnp.float32).T
    send(2, 0, owners)
    for slot in range(2):
        loads[2 * slot].wait()
        loads[2 * slot + 1].wait()
        for i in range(per_owner):
            columns = slice(i * owners, (i + 1) * owners)
            prod = raw[2 * slot, :, columns].astype(jnp.float32) * raw[
                2 * slot + 1, :, columns
            ].astype(jnp.float32)
            spread[slot, pl.ds(i, owners, stride=PITCH), :] = prod.T
        send(slot, 0, owners)


def pack(query, key, value, grad, filt, owners):
    tokens, channels = query.shape
    per_owner = channels // owners
    return pl.pallas_call(
        pack_kernel,
        in_specs=[pl.BlockSpec(memory_space=pltpu.HBM)] * 5,
        out_specs=pl.BlockSpec(memory_space=pltpu.VMEM),
        out_shape=jax.ShapeDtypeStruct((owners, 3, per_owner, LANES), jnp.bfloat16),
        scratch_shapes=[
            pltpu.VMEM((4, tokens, channels), jnp.bfloat16),
            pltpu.VMEM(filt.shape, jnp.bfloat16),
            pltpu.VMEM((3, owners * PITCH, LANES), jnp.float32),
            pltpu.SemaphoreType.DMA((5,)),
        ],
        compiler_params=pltpu.CompilerParams(vmem_limit_bytes=24 << 20),
    )(*[pltpu.with_memory_space_constraint(x, pltpu.HBM) for x in (query, key, value, grad, filt)])


def mix_kernel(blocks, outer_fwd, inner_fwd, inner_bwd, outer_bwd, cos, sin, out, wide, done):
    blocks_p, groups, _, per_owner, _ = blocks.shape
    rows = blocks_p * groups
    half = per_owner // 2
    for slot in range(2):
        lines = blocks[:, :, slot].astype(jnp.float32).reshape(rows, per_owner, LANES)
        wide[slot, :, :per_owner] = lines

    wide = wide.reshape(2, rows * PITCH, LANES)
    flat = done.reshape(2, rows * PITCH, LANES)

    def dot(left, right):
        return jnp.dot(left, right, preferred_element_type=jnp.float32)

    def step(group, carry):
        filt = blocks[:, group, 2].astype(jnp.float32)
        lines = [filt[:, j * half : (j + 1) * half].reshape(rows, LANES) for j in range(2)]
        for slot in range(2):
            for j in range(2):
                lines.append(wide[slot, pl.ds(2 * group + j, rows, stride=PITCH), :])
        mids = []
        for i in range(3):
            pair = jnp.concatenate(lines[2 * i : 2 * i + 2], axis=1).astype(jnp.bfloat16)
            mid = dot(outer_fwd[...], pair).reshape(rows // TILE, 2, TILE, 2 * LANES)
            mids += [mid[..., :LANES], mid[..., LANES:]]
        c, s = cos[...].reshape(rows // TILE, TILE, LANES), sin[...].reshape(rows // TILE, TILE, LANES)
        spun = []
        for mid in mids:
            real, imag = mid[:, 0], mid[:, 1]
            spun.append(jnp.concatenate(
                [real * c + imag * s, imag * c - real * s], axis=2
            ).reshape(rows, 2 * LANES).astype(jnp.bfloat16))
        spec = []
        for i in range(3):
            both = dot(jnp.concatenate(spun[2 * i : 2 * i + 2], axis=0), inner_fwd[...])
            spec += [(both[:rows, :LANES], both[:rows, LANES:]), (both[rows:, :LANES], both[rows:, LANES:])]
        mixed = []
        for slot in range(2):
            for j in range(2):
                (fr, fi), (gr, gi) = spec[j], spec[2 + 2 * slot + j]
                if slot == 0:
                    real, imag = fr * gr - fi * gi, fr * gi + fi * gr
                else:
                    real, imag = fr * gr + fi * gi, fr * gi - fi * gr
                mixed.append(jnp.concatenate([real, imag], axis=1).astype(jnp.bfloat16))
        boths = [dot(m, inner_bwd[...]) for m in mixed]
        spun = []
        for both in boths:
            both = both.reshape(rows // TILE, TILE, 2 * LANES)
            real, imag = both[..., :LANES], both[..., LANES:]
            spun.append(jnp.stack(
                [real * c - imag * s, real * s + imag * c], axis=1
            ).reshape(2 * rows, LANES).astype(jnp.bfloat16))
        for slot in range(2):
            result = dot(outer_bwd[...], jnp.concatenate(spun[2 * slot : 2 * slot + 2], axis=1))
            for j in range(2):
                flat[slot, pl.ds(2 * group + j, rows, stride=PITCH), :] = result[
                    :, j * LANES : (j + 1) * LANES
                ]
        return carry

    lax.fori_loop(0, groups, step, 0, unroll=True)
    for slot in range(2):
        out[:, slot] = done[slot, :, :per_owner].astype(jnp.bfloat16)


def mix(blocks, groups):
    rows, _, per_owner, _ = blocks.shape
    consts = [jnp.asarray(t) for t in tables(rows * LANES)]
    return pl.pallas_call(
        mix_kernel,
        out_shape=jax.ShapeDtypeStruct((rows, 2, per_owner, LANES), jnp.bfloat16),
        scratch_shapes=[
            pltpu.VMEM((2, rows, PITCH, LANES), jnp.float32),
            pltpu.VMEM((2, rows, PITCH, LANES), jnp.float32),
        ],
        compiler_params=pltpu.CompilerParams(vmem_limit_bytes=32 << 20),
    )(blocks.reshape(rows // groups, groups, 3, per_owner, LANES), *consts)


def gate_kernel(sums, query, key, value, grad, gated, grad_query, grad_key, grad_value, wide, ready, sems):
    owners, _, per_owner, _ = sums.shape
    channels = query.shape[1]
    width = 2 * owners
    uses = ((query, gated), (grad, grad_query)), ((value, grad_key), (key, grad_value))
    stores = []
    flat = wide.reshape(2, owners * PITCH, LANES)
    for slot in range(2):
        wide[slot, :, :per_owner] = sums[:, slot].astype(jnp.float32)
        for group in range(channels // width):
            for j in range(2):
                i = 2 * group + j
                columns = slice(i * owners, (i + 1) * owners)
                tokens = flat[slot, pl.ds(i, owners, stride=PITCH), :].T
                for k, (source, _) in enumerate(uses[slot]):
                    ready[2 * slot + k, :, columns] = (
                        source[:, columns].astype(jnp.float32) * tokens
                    ).astype(jnp.bfloat16)
            columns = pl.ds(group * width, width)
            for k, (_, target) in enumerate(uses[slot]):
                stores.append(
                    pltpu.make_async_copy(
                        ready.at[2 * slot + k, :, columns],
                        target.at[:, columns],
                        sems.at[len(stores)],
                    )
                )
                stores[-1].start()
    for store in stores:
        store.wait()


def gate(sums, query, key, value, grad, width):
    tokens, channels = query.shape
    owners, _, per_owner, _ = sums.shape
    whole = pl.BlockSpec(memory_space=pltpu.VMEM)
    return pl.pallas_call(
        gate_kernel,
        in_specs=[whole] * 5,
        out_specs=[pl.BlockSpec(memory_space=pltpu.HBM)] * 4,
        out_shape=[jax.ShapeDtypeStruct((tokens, channels), jnp.bfloat16)] * 4,
        scratch_shapes=[
            pltpu.VMEM((2, owners, PITCH, LANES), jnp.float32),
            pltpu.VMEM((4, tokens, channels), jnp.bfloat16),
            pltpu.SemaphoreType.DMA((4 * channels // width,)),
        ],
        compiler_params=pltpu.CompilerParams(vmem_limit_bytes=24 << 20),
    )(sums, query, key, value, grad)


def body(query_in, key_in, value_in, grad_out, filters):
    axes = ("dp", "ctx")
    groups = lax.axis_size("ctx")
    owners = lax.axis_size("dp") * groups
    packed = pack(query_in, key_in, value_in, grad_out, filters, owners)
    blocks = lax.all_to_all(packed, axes, split_axis=0, concat_axis=0, tiled=True)
    mixed = mix(blocks, groups)
    sums = lax.all_to_all(mixed, axes, split_axis=0, concat_axis=0, tiled=True)
    return tuple(gate(sums, query_in, key_in, value_in, grad_out, filters.shape[1]))


def solution(mesh):
    tokens = P(("dp", "ctx"), None)
    return jax.shard_map(
        body,
        mesh=mesh,
        in_specs=(tokens, tokens, tokens, tokens, P("dp", "ctx")),
        out_specs=(tokens, tokens, tokens, tokens),
        check_vma=False,
    )
```

```python
import jax
import jax.numpy as jnp
import ml_dtypes
import numpy as np
from jax import lax
from jax.experimental import pallas as pl
from jax.experimental.pallas import tpu as pltpu
from jax.sharding import PartitionSpec as P

LANES = 128
TILE = 16
PITCH = 24


def tables(length):
    rows = length // LANES
    period = 2 * length
    freq = np.arange(rows) + 0.5
    outer = 2.0 * np.pi / (2 * rows) * np.outer(freq, np.arange(rows))
    inner = 2.0 * np.pi / LANES * (np.outer(np.arange(LANES), np.arange(LANES)) % LANES)
    spin = 2.0 * np.pi / period * np.outer(freq, np.arange(LANES))
    cos, sin = np.cos(inner), np.sin(inner)
    kind = ml_dtypes.bfloat16
    both = np.stack([np.cos(outer), -np.sin(outer)], axis=1)
    both = both.reshape(rows // TILE, TILE, 2, rows).transpose(0, 2, 1, 3).reshape(2 * rows, rows)
    outer_fwd = both.astype(kind)
    inner_fwd = np.block([[cos, -sin], [sin, cos]]).astype(kind)
    inner_bwd = np.block([[cos, sin], [-sin, cos]]).astype(kind)
    scale = np.float32(2.0 / period)
    outer_bwd = (both.T.astype(kind).astype(np.float32) * scale).astype(kind)
    spin_cos = np.cos(spin).astype(np.float32)
    spin_sin = np.sin(spin).astype(np.float32)
    return outer_fwd, inner_fwd, inner_bwd, outer_bwd, spin_cos, spin_sin


def turned(block):
    size = block.shape[0]
    eye = (
        lax.broadcasted_iota(jnp.int32, (size, size), 0)
        == lax.broadcasted_iota(jnp.int32, (size, size), 1)
    ).astype(jnp.bfloat16)
    return lax.dot_general(
        block, eye, (((0,), (0,)), ((), ())), preferred_element_type=jnp.float32
    )


def pack_kernel(query, key, value, grad, filt, out, raw, raw_filt, spread, sems):
    owners, _, per_owner, _ = out.shape
    half = per_owner // 2
    load_filt = pltpu.make_async_copy(filt, raw_filt, sems.at[4])
    load_filt.start()
    loads = []
    for i, source in enumerate((key, value, grad, query)):
        loads.append(pltpu.make_async_copy(source, raw.at[i], sems.at[i]))
        loads[-1].start()

    def send(slot, first, count):
        some = slice(first, first + count)
        lines = spread[slot, first * PITCH : (first + count) * PITCH]
        lines = lines.reshape(count, PITCH, LANES)[:, :per_owner]
        out[some, slot] = lines.astype(jnp.bfloat16)

    load_filt.wait()
    for j in range(2):
        for a in range(half):
            lines = raw_filt[a * LANES : (a + 1) * LANES, j * owners : (j + 1) * owners]
            spread[2, pl.ds(j * half + a, owners, stride=PITCH), :] = turned(lines)
    send(2, 0, owners)
    for slot in range(2):
        loads[2 * slot].wait()
        loads[2 * slot + 1].wait()
        for i in range(per_owner):
            columns = slice(i * owners, (i + 1) * owners)
            prod = raw[2 * slot, :, columns].astype(jnp.float32) * raw[
                2 * slot + 1, :, columns
            ].astype(jnp.float32)
            spread[slot, pl.ds(i, owners, stride=PITCH), :] = turned(prod.astype(jnp.bfloat16))
        send(slot, 0, owners)


def pack(query, key, value, grad, filt, owners):
    tokens, channels = query.shape
    per_owner = channels // owners
    return pl.pallas_call(
        pack_kernel,
        in_specs=[pl.BlockSpec(memory_space=pltpu.HBM)] * 5,
        out_specs=pl.BlockSpec(memory_space=pltpu.VMEM),
        out_shape=jax.ShapeDtypeStruct((owners, 3, per_owner, LANES), jnp.bfloat16),
        scratch_shapes=[
            pltpu.VMEM((4, tokens, channels), jnp.bfloat16),
            pltpu.VMEM(filt.shape, jnp.bfloat16),
            pltpu.VMEM((3, (owners + 1) * PITCH, LANES), jnp.float32),
            pltpu.SemaphoreType.DMA((5,)),
        ],
        compiler_params=pltpu.CompilerParams(vmem_limit_bytes=24 << 20),
    )(*[pltpu.with_memory_space_constraint(x, pltpu.HBM) for x in (query, key, value, grad, filt)])


def mix_kernel(blocks, outer_fwd, inner_fwd, inner_bwd, outer_bwd, cos, sin, out, wide, done):
    blocks_p, groups, _, per_owner, _ = blocks.shape
    rows = blocks_p * groups
    half = per_owner // 2
    for slot in range(2):
        lines = blocks[:, :, slot].astype(jnp.float32).reshape(rows, per_owner, LANES)
        wide[slot, :rows, :per_owner] = lines

    wide = wide.reshape(2, (rows + 1) * PITCH, LANES)
    flat = done.reshape(2, (rows + 1) * PITCH, LANES)

    def dot(left, right):
        return jnp.dot(left, right, preferred_element_type=jnp.float32)

    def step(group, carry):
        c, s = cos[...].reshape(rows // TILE, TILE, LANES), sin[...].reshape(rows // TILE, TILE, LANES)
        filt = blocks[:, group, 2].astype(jnp.float32)
        lines = [filt[:, j * half : (j + 1) * half].reshape(rows, LANES) for j in range(2)]
        for slot in range(2):
            for j in range(2):
                lines.append(wide[slot, pl.ds(2 * group + j, rows, stride=PITCH), :])

        def spin(mid):
            real, imag = mid[:, 0], mid[:, 1]
            return jnp.concatenate(
                [real * c + imag * s, imag * c - real * s], axis=2
            ).reshape(rows, 2 * LANES).astype(jnp.bfloat16)

        def back(both):
            both = both.reshape(rows // TILE, TILE, 2 * LANES)
            real, imag = both[..., :LANES], both[..., LANES:]
            return jnp.stack(
                [real * c - imag * s, real * s + imag * c], axis=1
            ).reshape(2 * rows, LANES).astype(jnp.bfloat16)

        def times(slot, j):
            (fr, fi), (gr, gi) = spec[j], spec[2 + 2 * slot + j]
            if slot == 0:
                real, imag = fr * gr - fi * gi, fr * gi + fi * gr
            else:
                real, imag = fr * gr + fi * gi, fr * gi - fi * gr
            return jnp.concatenate([real, imag], axis=1).astype(jnp.bfloat16)

        def finish(slot, spun):
            result = dot(outer_bwd[...], jnp.concatenate(spun, axis=1))
            for j in range(2):
                flat[slot, pl.ds(2 * group + j, rows, stride=PITCH), :] = result[
                    :, j * LANES : (j + 1) * LANES
                ]

        mids, spun, spec = {}, {}, {}
        for i in (0, 1, 2):
            pair = jnp.concatenate(lines[2 * i : 2 * i + 2], axis=1).astype(jnp.bfloat16)
            mid = dot(outer_fwd[...], pair).reshape(rows // TILE, 2, TILE, 2 * LANES)
            mids[2 * i], mids[2 * i + 1] = mid[..., :LANES], mid[..., LANES:]
        for i in (0, 1, 2):
            spun[2 * i], spun[2 * i + 1] = spin(mids[2 * i]), spin(mids[2 * i + 1])
        for i in (0, 1, 2):
            both = dot(jnp.concatenate([spun[2 * i], spun[2 * i + 1]], axis=0), inner_fwd[...])
            spec[2 * i] = both[:rows, :LANES], both[:rows, LANES:]
            spec[2 * i + 1] = both[rows:, :LANES], both[rows:, LANES:]
        mixed = [times(slot, j) for slot in range(2) for j in range(2)]
        boths = [dot(part, inner_bwd[...]) for part in mixed]
        for slot in range(2):
            finish(slot, [back(boths[2 * slot]), back(boths[2 * slot + 1])])
        return carry

    lax.fori_loop(0, groups, step, 0, unroll=True)
    for slot in range(2):
        out[:, slot] = done[slot, :rows, :per_owner].astype(jnp.bfloat16)


def mix(blocks, groups):
    rows, _, per_owner, _ = blocks.shape
    consts = [jnp.asarray(t) for t in tables(rows * LANES)]
    return pl.pallas_call(
        mix_kernel,
        out_shape=jax.ShapeDtypeStruct((rows, 2, per_owner, LANES), jnp.bfloat16),
        scratch_shapes=[
            pltpu.VMEM((2, rows + 1, PITCH, LANES), jnp.float32),
            pltpu.VMEM((2, rows + 1, PITCH, LANES), jnp.float32),
        ],
        compiler_params=pltpu.CompilerParams(vmem_limit_bytes=32 << 20),
    )(blocks.reshape(rows // groups, groups, 3, per_owner, LANES), *consts)


def gate_kernel(sums, query, key, value, grad, gated, grad_query, grad_key, grad_value, wide, ready, sems):
    owners, _, per_owner, _ = sums.shape
    channels = query.shape[1]
    width = 2 * owners
    uses = ((query, gated), (grad, grad_query)), ((value, grad_key), (key, grad_value))
    stores = []
    flat = wide.reshape(2, (owners + 1) * PITCH, LANES)
    for slot in range(2):
        wide[slot, :owners, :per_owner] = sums[:, slot].astype(jnp.float32)
        for group in range(channels // width):
            for j in range(2):
                i = 2 * group + j
                columns = slice(i * owners, (i + 1) * owners)
                tokens = flat[slot, pl.ds(i, owners, stride=PITCH), :].T
                for k, (source, _) in enumerate(uses[slot]):
                    ready[2 * slot + k, :, columns] = (
                        source[:, columns].astype(jnp.float32) * tokens
                    ).astype(jnp.bfloat16)
            columns = pl.ds(group * width, width)
            for k, (_, target) in enumerate(uses[slot]):
                stores.append(
                    pltpu.make_async_copy(
                        ready.at[2 * slot + k, :, columns],
                        target.at[:, columns],
                        sems.at[len(stores)],
                    )
                )
                stores[-1].start()
    for store in stores:
        store.wait()


def gate(sums, query, key, value, grad, width):
    tokens, channels = query.shape
    owners, _, per_owner, _ = sums.shape
    whole = pl.BlockSpec(memory_space=pltpu.VMEM)
    return pl.pallas_call(
        gate_kernel,
        in_specs=[whole] * 5,
        out_specs=[pl.BlockSpec(memory_space=pltpu.HBM)] * 4,
        out_shape=[jax.ShapeDtypeStruct((tokens, channels), jnp.bfloat16)] * 4,
        scratch_shapes=[
            pltpu.VMEM((2, owners + 1, PITCH, LANES), jnp.float32),
            pltpu.VMEM((4, tokens, channels), jnp.bfloat16),
            pltpu.SemaphoreType.DMA((4 * channels // width,)),
        ],
        compiler_params=pltpu.CompilerParams(vmem_limit_bytes=24 << 20),
    )(sums, query, key, value, grad)


def body(query_in, key_in, value_in, grad_out, filters):
    axes = ("dp", "ctx")
    groups = lax.axis_size("ctx")
    owners = lax.axis_size("dp") * groups
    packed = pack(query_in, key_in, value_in, grad_out, filters, owners)
    blocks = lax.all_to_all(packed, axes, split_axis=0, concat_axis=0, tiled=True)
    mixed = mix(blocks, groups)
    sums = lax.all_to_all(mixed, axes, split_axis=0, concat_axis=0, tiled=True)
    return tuple(gate(sums, query_in, key_in, value_in, grad_out, filters.shape[1]))


def solution(mesh):
    tokens = P(("dp", "ctx"), None)
    return jax.shard_map(
        body,
        mesh=mesh,
        in_specs=(tokens, tokens, tokens, tokens, P("dp", "ctx")),
        out_specs=(tokens, tokens, tokens, tokens),
        check_vma=False,
    )
```

```python
import jax
import jax.numpy as jnp
import ml_dtypes
import numpy as np
from jax import lax
from jax.experimental import pallas as pl
from jax.experimental.pallas import tpu as pltpu
from jax.sharding import PartitionSpec as P

LANES = 128
TILE = 16
PITCH = 24


def tables(length):
    rows = length // LANES
    period = 2 * length
    freq = np.arange(rows) + 0.5
    outer = 2.0 * np.pi / (2 * rows) * np.outer(freq, np.arange(rows))
    inner = 2.0 * np.pi / LANES * (np.outer(np.arange(LANES), np.arange(LANES)) % LANES)
    spin = 2.0 * np.pi / period * np.outer(freq, np.arange(LANES))
    cos, sin = np.cos(inner), np.sin(inner)
    kind = ml_dtypes.bfloat16
    both = np.stack([np.cos(outer), -np.sin(outer)], axis=1)
    both = both.reshape(rows // TILE, TILE, 2, rows).transpose(0, 2, 1, 3).reshape(2 * rows, rows)
    outer_fwd = both.astype(kind)
    inner_fwd = np.block([[cos, -sin], [sin, cos]]).astype(kind)
    inner_bwd = np.block([[cos, sin], [-sin, cos]]).astype(kind)
    scale = np.float32(2.0 / period)
    outer_bwd = (both.T.astype(kind).astype(np.float32) * scale).astype(kind)
    spin_cos = np.cos(spin).astype(np.float32)
    spin_sin = np.sin(spin).astype(np.float32)
    return outer_fwd, inner_fwd, inner_bwd, outer_bwd, spin_cos, spin_sin


def turned(block):
    size = block.shape[0]
    eye = (
        lax.broadcasted_iota(jnp.int32, (size, size), 0)
        == lax.broadcasted_iota(jnp.int32, (size, size), 1)
    ).astype(jnp.bfloat16)
    return lax.dot_general(
        block, eye, (((0,), (0,)), ((), ())), preferred_element_type=jnp.float32
    )


def pack_kernel(query, key, value, grad, filt, out, raw, raw_filt, spread, sems):
    owners, _, per_owner, _ = out.shape
    half = per_owner // 2
    load_filt = pltpu.make_async_copy(filt, raw_filt, sems.at[4])
    load_filt.start()
    loads = []
    for i, source in enumerate((key, value, grad, query)):
        loads.append(pltpu.make_async_copy(source, raw.at[i], sems.at[i]))
        loads[-1].start()

    def send(slot, first, count):
        some = slice(first, first + count)
        lines = spread[slot, first * PITCH : (first + count) * PITCH]
        lines = lines.reshape(count, PITCH, LANES)[:, :per_owner]
        out[some, slot] = lines.astype(jnp.bfloat16)

    load_filt.wait()
    for j in range(2):
        for a in range(half):
            lines = raw_filt[a * LANES : (a + 1) * LANES, j * owners : (j + 1) * owners]
            spread[2, pl.ds(j * half + a, owners, stride=PITCH), :] = turned(lines)
    send(2, 0, owners)
    for slot in range(2):
        loads[2 * slot].wait()
        loads[2 * slot + 1].wait()
        for i in range(per_owner):
            columns = slice(i * owners, (i + 1) * owners)
            prod = raw[2 * slot, :, columns] * raw[2 * slot + 1, :, columns]
            spread[slot, pl.ds(i, owners, stride=PITCH), :] = turned(prod)
        send(slot, 0, owners)


def pack(query, key, value, grad, filt, owners):
    tokens, channels = query.shape
    per_owner = channels // owners
    return pl.pallas_call(
        pack_kernel,
        in_specs=[pl.BlockSpec(memory_space=pltpu.HBM)] * 5,
        out_specs=pl.BlockSpec(memory_space=pltpu.VMEM),
        out_shape=jax.ShapeDtypeStruct((owners, 3, per_owner, LANES), jnp.bfloat16),
        scratch_shapes=[
            pltpu.VMEM((4, tokens, channels), jnp.bfloat16),
            pltpu.VMEM(filt.shape, jnp.bfloat16),
            pltpu.VMEM((3, (owners + 1) * PITCH, LANES), jnp.float32),
            pltpu.SemaphoreType.DMA((5,)),
        ],
        compiler_params=pltpu.CompilerParams(vmem_limit_bytes=24 << 20),
    )(*[pltpu.with_memory_space_constraint(x, pltpu.HBM) for x in (query, key, value, grad, filt)])


def mix_kernel(blocks, outer_fwd, inner_fwd, inner_bwd, outer_bwd, cos, sin, out, wide, done):
    blocks_p, groups, _, per_owner, _ = blocks.shape
    rows = blocks_p * groups
    half = per_owner // 2
    for slot in range(2):
        lines = blocks[:, :, slot].astype(jnp.float32).reshape(rows, per_owner, LANES)
        wide[slot, :rows, :per_owner] = lines

    wide = wide.reshape(2, (rows + 1) * PITCH, LANES)
    flat = done.reshape(2, (rows + 1) * PITCH, LANES)

    def dot(left, right):
        return jnp.dot(left, right, preferred_element_type=jnp.float32)

    def step(group, carry):
        c, s = cos[...].reshape(rows // TILE, TILE, LANES), sin[...].reshape(rows // TILE, TILE, LANES)
        filt = blocks[:, group, 2].astype(jnp.float32)
        lines = [filt[:, j * half : (j + 1) * half].reshape(rows, LANES) for j in range(2)]
        for slot in range(2):
            for j in range(2):
                lines.append(wide[slot, pl.ds(2 * group + j, rows, stride=PITCH), :])

        def spin(mid):
            real, imag = mid[:, 0], mid[:, 1]
            return jnp.concatenate(
                [real * c + imag * s, imag * c - real * s], axis=2
            ).reshape(rows, 2 * LANES).astype(jnp.bfloat16)

        def back(both):
            both = both.reshape(rows // TILE, TILE, 2 * LANES)
            real, imag = both[..., :LANES], both[..., LANES:]
            return jnp.stack(
                [real * c - imag * s, real * s + imag * c], axis=1
            ).reshape(2 * rows, LANES).astype(jnp.bfloat16)

        def times(slot, j):
            (fr, fi), (gr, gi) = spec[j], spec[2 + 2 * slot + j]
            if slot == 0:
                real, imag = fr * gr - fi * gi, fr * gi + fi * gr
            else:
                real, imag = fr * gr + fi * gi, fr * gi - fi * gr
            return jnp.concatenate([real, imag], axis=1).astype(jnp.bfloat16)

        def finish(slot, spun):
            result = dot(outer_bwd[...], jnp.concatenate(spun, axis=1))
            for j in range(2):
                flat[slot, pl.ds(2 * group + j, rows, stride=PITCH), :] = result[
                    :, j * LANES : (j + 1) * LANES
                ]

        mids, spun, spec = {}, {}, {}
        for i in (0, 1, 2):
            pair = jnp.concatenate(lines[2 * i : 2 * i + 2], axis=1).astype(jnp.bfloat16)
            mid = dot(outer_fwd[...], pair).reshape(rows // TILE, 2, TILE, 2 * LANES)
            mids[2 * i], mids[2 * i + 1] = mid[..., :LANES], mid[..., LANES:]
        for i in (0, 1, 2):
            spun[2 * i], spun[2 * i + 1] = spin(mids[2 * i]), spin(mids[2 * i + 1])
        for i in (0, 1, 2):
            both = dot(jnp.concatenate([spun[2 * i], spun[2 * i + 1]], axis=0), inner_fwd[...])
            spec[2 * i] = both[:rows, :LANES], both[:rows, LANES:]
            spec[2 * i + 1] = both[rows:, :LANES], both[rows:, LANES:]
        mixed = [times(slot, j) for slot in range(2) for j in range(2)]
        boths = [dot(part, inner_bwd[...]) for part in mixed]
        for slot in range(2):
            finish(slot, [back(boths[2 * slot]), back(boths[2 * slot + 1])])
        return carry

    lax.fori_loop(0, groups, step, 0, unroll=True)
    for slot in range(2):
        out[:, slot] = done[slot, :rows, :per_owner].astype(jnp.bfloat16)


def mix(blocks, groups):
    rows, _, per_owner, _ = blocks.shape
    consts = [jnp.asarray(t) for t in tables(rows * LANES)]
    return pl.pallas_call(
        mix_kernel,
        out_shape=jax.ShapeDtypeStruct((rows, 2, per_owner, LANES), jnp.bfloat16),
        scratch_shapes=[
            pltpu.VMEM((2, rows + 1, PITCH, LANES), jnp.float32),
            pltpu.VMEM((2, rows + 1, PITCH, LANES), jnp.float32),
        ],
        compiler_params=pltpu.CompilerParams(vmem_limit_bytes=32 << 20),
    )(blocks.reshape(rows // groups, groups, 3, per_owner, LANES), *consts)


def gate_kernel(sums, query, key, value, grad, gated, grad_query, grad_key, grad_value, wide, ready, sems):
    owners, _, per_owner, _ = sums.shape
    channels = query.shape[1]
    width = 2 * owners
    uses = ((query, gated), (grad, grad_query)), ((value, grad_key), (key, grad_value))
    stores = []
    flat = wide.reshape(2, (owners + 1) * PITCH, LANES)
    for slot in range(2):
        wide[slot, :owners, :per_owner] = sums[:, slot].astype(jnp.float32)
        for group in range(channels // width):
            for j in range(2):
                i = 2 * group + j
                columns = slice(i * owners, (i + 1) * owners)
                tokens = flat[slot, pl.ds(i, owners, stride=PITCH), :].T.astype(jnp.bfloat16)
                for k, (source, _) in enumerate(uses[slot]):
                    ready[2 * slot + k, :, columns] = source[:, columns] * tokens
            columns = pl.ds(group * width, width)
            for k, (_, target) in enumerate(uses[slot]):
                stores.append(
                    pltpu.make_async_copy(
                        ready.at[2 * slot + k, :, columns],
                        target.at[:, columns],
                        sems.at[len(stores)],
                    )
                )
                stores[-1].start()
    for store in stores:
        store.wait()


def gate(sums, query, key, value, grad, width):
    tokens, channels = query.shape
    owners, _, per_owner, _ = sums.shape
    whole = pl.BlockSpec(memory_space=pltpu.VMEM)
    return pl.pallas_call(
        gate_kernel,
        in_specs=[whole] * 5,
        out_specs=[pl.BlockSpec(memory_space=pltpu.HBM)] * 4,
        out_shape=[jax.ShapeDtypeStruct((tokens, channels), jnp.bfloat16)] * 4,
        scratch_shapes=[
            pltpu.VMEM((2, owners + 1, PITCH, LANES), jnp.float32),
            pltpu.VMEM((4, tokens, channels), jnp.bfloat16),
            pltpu.SemaphoreType.DMA((4 * channels // width,)),
        ],
        compiler_params=pltpu.CompilerParams(vmem_limit_bytes=24 << 20),
    )(sums, query, key, value, grad)


def body(query_in, key_in, value_in, grad_out, filters):
    axes = ("dp", "ctx")
    groups = lax.axis_size("ctx")
    owners = lax.axis_size("dp") * groups
    packed = pack(query_in, key_in, value_in, grad_out, filters, owners)
    blocks = lax.all_to_all(packed, axes, split_axis=0, concat_axis=0, tiled=True)
    mixed = mix(blocks, groups)
    sums = lax.all_to_all(mixed, axes, split_axis=0, concat_axis=0, tiled=True)
    return tuple(gate(sums, query_in, key_in, value_in, grad_out, filters.shape[1]))


def solution(mesh):
    tokens = P(("dp", "ctx"), None)
    return jax.shard_map(
        body,
        mesh=mesh,
        in_specs=(tokens, tokens, tokens, tokens, P("dp", "ctx")),
        out_specs=(tokens, tokens, tokens, tokens),
        check_vma=False,
    )
```
